256 devices in a mesh: kvh: 8 (over x, core), tok: 32 (over z, y).
Axes of the slice: x: 4, y: 4, z: 8, core: 2. Of those that a mesh axis runs over, the one named last changes fastest.
Arguments:
- token_ids: int32 [128], replicated, may hold values from 0 to 64127
- lengths: int32 [128], replicated, may hold values from 1 to 1024, 65536 in all
- embed_table: bfloat16 [64128, 8192], P('kvh', 'tok'), may hold values from -2500 to 2500
- norm_gain: bfloat16 [8192], P('tok'), may hold values from 0.099609375 to 1.8984375
- w_query: bfloat16 [8192, 8192], P('tok', 'kvh'), may hold values from -0.0625 to 0.0625
- w_key: bfloat16 [8192, 1024], P('tok', 'kvh'), may hold values from -0.0625 to 0.0625
- w_value: bfloat16 [8192, 1024], P('tok', 'kvh'), may hold values from -0.0625 to 0.0625
- prefix_keys: bfloat16 [8, 262144, 128], P('kvh', 'tok'), may hold values from -1000 to 1000
- prefix_values: bfloat16 [8, 262144, 128], P('kvh', 'tok'), may hold values from -10 to 10
- suffix_keys: bfloat16 [128, 8, 1024, 128], P('tok', 'kvh'), may hold values from -14 to 14
- suffix_values: bfloat16 [128, 8, 1024, 128], P('tok', 'kvh'), may hold values from -6 to 6
- w_out: bfloat16 [8192, 8192], P('kvh', 'tok'), may hold values from -0.0625 to 0.0625
Outputs:
- context: bfloat16 [128, 8192], P('tok', 'kvh')
- attn_out: bfloat16 [128, 8192], P('kvh', 'tok')
- new_keys: bfloat16 [128, 1024], P('tok', 'kvh')
- new_values: bfloat16 [128, 1024], P('tok', 'kvh')
The draws below stay inside these ranges and needn't reach their ends.
Inputs may be any that keep to these rules, and one draw needn't show every extreme that they name: Cached suffix tokens of each request: slots 0 to lengths - 1 of its suffix cache hold data; the largest is 1024.
All inputs are finite; a program needn't handle non-finite values.
Results may differ from the reference program's by a relative error of at most 0.025.
Values may be sent and summed in bfloat16 or wider, within the bound.
No kernel may reach another device: no remote copies, remote signals or barrier semaphores. Data moves between devices by JAX's collectives and lax.ppermute only.
A program may use at most 128 MiB of HBM per device.

```python
import math
import jax
import jax.numpy as jnp
import numpy as np
from jax import lax

D = 8192
HD = 128
GROUP = 8
KVH = 8
H = 64
VOCAB = 64128
REQ = 128
PRE_DEV = 8192
PREFIX = 262144
SUF = 1024
N_TOK = 32


def draw_embed_table(key, part):
    key = jax.random.fold_in(key, 21)
    noise_key, row_key, col_key = jax.random.split(key, 3)
    column_place = jnp.arange(D, dtype=jnp.float32)[None, :] / D
    row_scale = jnp.exp(jax.random.uniform(row_key, (VOCAB, 1), dtype=jnp.float32) * math.log(10.0))
    jitter = jax.random.uniform(col_key, (1, D), dtype=jnp.float32, minval=-0.3, maxval=0.3)
    base = jnp.clip(jax.random.normal(noise_key, (VOCAB, D), dtype=jnp.float32), -6.0, 6.0)
    col_scale = jnp.exp(column_place * math.log(10.0) + jitter)
    return (base * row_scale * col_scale).astype(jnp.bfloat16)


def draw_prefix_keys(key, part):
    key = jax.random.fold_in(key, 22)
    noise_key, scale_key = jax.random.split(key, 2)
    row_scale = 0.1 * jnp.exp(jax.random.uniform(scale_key, (KVH, PREFIX, 1), dtype=jnp.float32) * math.log(10.0))
    base = jnp.clip(jax.random.normal(noise_key, (KVH, PREFIX, HD), dtype=jnp.float32), -6.0, 6.0)
    result = base * row_scale
    return result.astype(jnp.bfloat16)


def draw_prefix_values(key, part):
    key = jax.random.fold_in(key, 23)
    noise_key, freq_key, phase_key = jax.random.split(key, 3)
    place = jnp.arange(PREFIX, dtype=jnp.float32)[None, :, None] / PREFIX
    freq = jax.random.randint(freq_key, (KVH, 1, HD), 1, 9).astype(jnp.float32)
    phase = jax.random.uniform(phase_key, (KVH, 1, HD), dtype=jnp.float32, minval=-math.pi, maxval=math.pi)
    base = jnp.clip(jax.random.normal(noise_key, (KVH, PREFIX, HD), dtype=jnp.float32), -6.0, 6.0)
    amplitude = 3.0
    return (base + amplitude * jnp.cos(2.0 * math.pi * freq * place + phase)).astype(jnp.bfloat16)


def with_ends(values, stream_key, low, high):
    dims = values.shape
    index_at = [jax.random.randint(jax.random.fold_in(stream_key, axis), (), 0, dims[axis]) for axis in range(len(dims))]
    values = values.at[tuple(index_at)].set(low)
    longest = dims.index(max(dims))
    index_at[longest] = (index_at[longest] + 1) % dims[longest]
    return values.at[tuple(index_at)].set(high)


def steps_of(rng, shape, pieces, low, high):
    factor_of = 1.0
    for position, parts in pieces:
        draws = jax.random.uniform(jax.random.fold_in(jax.random.fold_in(rng, 6), position), (parts,), jnp.float32, low / len(pieces), high / len(pieces))
        factor_of = factor_of * jnp.repeat(jnp.exp(draws), shape[position] // parts).reshape((-1,) + (1,) * (len(shape) - 1 - position))
    return factor_of


def cumulative_ranks(amount, slope):
    weights = [(1 << 20) // math.isqrt(rank ** slope) + 1 for rank in range(1, amount + 1)]
    spread = 1 + sum(weights) // (1 << 30)
    return np.cumsum(np.array([max(1, weight // spread) for weight in weights]))


def skewed_ids(own_key, extent, count, slope):
    listing = cumulative_ranks(count, slope)
    lot = jax.random.randint(jax.random.fold_in(own_key, 1), extent, 0, int(listing[count - 1]))
    grade = jnp.searchsorted(jnp.asarray(listing, jnp.int32), lot, side="right")
    return jax.random.permutation(jax.random.fold_in(own_key, 2), count)[grade].astype(jnp.int32)


def length_profile(amount, total, most, skew):
    loads = [(1 << 20) // math.isqrt(grade ** skew) + 1 for grade in range(2, amount + 1)]
    rest, holding = total - most - (amount - 1), [1] * (amount - 1)
    while rest > 0:
        candidates = [i for i in range(amount - 1) if holding[i] < most]
        mass, remaining = sum([loads[i] for i in candidates]), rest
        for i in candidates:
            addition = min(most - holding[i], max(1, remaining * loads[i] // mass), rest)
            holding[i] = holding[i] + addition
            rest = rest - addition
    return np.array([most] + holding)


def ragged(own_key, count, total, most, lean):
    if count == 2:
        one = jax.random.randint(own_key, (), max(1, total - most), min(most, total - 1) + 1)
        return jnp.stack([one, total - one])
    sizes = jnp.asarray(length_profile(count, total, most, lean), jnp.int32)
    couples = (count - 1) // 2
    giver, sink = sizes[1:1 + 2 * couples:2], sizes[2:2 + 2 * couples:2]
    room = jnp.minimum(giver - 1, most - sink)
    moved = jax.random.randint(jax.random.fold_in(own_key, 1), (couples,), 0, 1 << 20) % (room + 1)
    sizes = sizes.at[1:1 + 2 * couples:2].set(giver - moved).at[2:2 + 2 * couples:2].set(sink + moved)
    return sizes[jax.random.permutation(jax.random.fold_in(own_key, 2), count)]


def scatter_about(key, extent, deviation, most, shards=(), kind=jnp.bfloat16):
    drawn = jax.random.normal(key, extent, jnp.float32) * deviation
    if len(shards) > 0:
        drawn = steps_of(key, extent, shards, -0.22, 0.18) * drawn
    return jnp.clip(drawn, min=-most, max=most).astype(kind)


def setup_inputs(seed: int = 0) -> dict:
    splits = jax.random.split(jax.random.key(seed), 13)
    return {
        "token_ids": with_ends(skewed_ids(splits[0], (REQ,), VOCAB, 2), jax.random.fold_in(splits[0], 3), 0, VOCAB - 1).astype(jnp.int32),
        "lengths": ragged(splits[1], REQ, REQ * SUF // 2, SUF, 2).astype(jnp.int32),
        "embed_table": draw_embed_table(jax.random.fold_in(splits[12], 71), 0),
        "norm_gain": jnp.clip(1.0 + 0.18 * jax.random.normal(splits[3], (D,), jnp.float32), 0.099609375, 1.8984375).astype(jnp.bfloat16),
        "w_query": scatter_about(splits[4], (D, H * HD), D ** -0.5, 0.0625, ((0, 32), (1, 8))),
        "w_key": scatter_about(splits[5], (D, KVH * HD), D ** -0.5, 0.0625, ((0, 32), (1, 8))),
        "w_value": scatter_about(splits[6], (D, KVH * HD), D ** -0.5, 0.0625, ((0, 32), (1, 8))),
        "prefix_keys": draw_prefix_keys(jax.random.fold_in(splits[12], 71), 0),
        "prefix_values": draw_prefix_values(jax.random.fold_in(splits[12], 71), 0),
        "suffix_keys": scatter_about(splits[9], (REQ, KVH, SUF, HD), 3.5, 14.0, ((0, 32), (1, 8))),
        "suffix_values": scatter_about(splits[10], (REQ, KVH, SUF, HD), 1.0, 6.0, ((0, 32), (1, 8))),
        "w_out": scatter_about(splits[11], (H * HD, D), (H * HD) ** -0.5, 0.0625, ((0, 8), (1, 32))),
    }


def round_trip(values_in):
    return lax.optimization_barrier(values_in.astype(jnp.bfloat16)).astype(jnp.float32)

def reference(token_ids, lengths, embed_table, norm_gain, w_query, w_key, w_value, prefix_keys, prefix_values, suffix_keys, suffix_values, w_out):
    tok_rows = jnp.take(embed_table, token_ids, axis=0)
    rows_float = tok_rows.astype(jnp.float32)
    inv_rms = lax.rsqrt(lax.optimization_barrier(jnp.mean(rows_float * rows_float, axis=1)) + 1e-05)
    scaled = (rows_float * norm_gain.astype(jnp.float32)).astype(jnp.bfloat16)
    queries = (jnp.dot(scaled, w_query, preferred_element_type=jnp.float32) * inv_rms[:, None]).astype(jnp.bfloat16)
    new_keys = (jnp.dot(scaled, w_key, preferred_element_type=jnp.float32) * inv_rms[:, None]).astype(jnp.bfloat16)
    new_values = (jnp.dot(scaled, w_value, preferred_element_type=jnp.float32) * inv_rms[:, None]).astype(jnp.bfloat16)
    score_scale = 1.0 / math.sqrt(HD)
    positions = jnp.arange(SUF, dtype=jnp.int32)
    suffix_valid = positions[None, None, :] < lengths.astype(jnp.int32)[:, None, None]

    def one_group(group_index):
        query_group = lax.dynamic_slice_in_dim(queries, group_index * GROUP * HD, GROUP * HD, 1).reshape(REQ, GROUP, HD).astype(jnp.float32)
        key_new = lax.dynamic_slice_in_dim(new_keys, group_index * HD, HD, 1).astype(jnp.float32)
        value_new = lax.dynamic_slice_in_dim(new_values, group_index * HD, HD, 1).astype(jnp.float32)
        key_blocks = prefix_keys[group_index].reshape(N_TOK, PRE_DEV, HD)
        value_blocks = prefix_values[group_index].reshape(N_TOK, PRE_DEV, HD)
        suffix_key = suffix_keys[:, group_index].astype(jnp.float32)
        suffix_value = suffix_values[:, group_index].astype(jnp.float32)

        def block_scores(key_block):
            return jnp.einsum('rgd,kd->rgk', query_group, key_block.astype(jnp.float32)) * score_scale

        def max_step(running, key_block):
            return (jnp.maximum(running, lax.optimization_barrier(jnp.max(block_scores(key_block), axis=2))), None)
        suffix_scores = jnp.einsum('rgd,rkd->rgk', query_group, suffix_key) * score_scale
        own_scores = jnp.einsum('rgd,rd->rg', query_group, key_new) * score_scale
        start_top = jnp.maximum(lax.optimization_barrier(jnp.max(jnp.where(suffix_valid, suffix_scores, -1e+30), axis=2)), own_scores)
        row_top, _ = lax.scan(max_step, start_top, key_blocks)

        def sum_step(carry_pair, block_pair):
            weight_total, weighted = carry_pair
            key_block, value_block = block_pair
            weights = jnp.exp(block_scores(key_block) - row_top[:, :, None])
            weighted = weighted + jnp.einsum('rgk,kd->rgd', round_trip(weights), value_block.astype(jnp.float32))
            return ((weight_total + lax.optimization_barrier(jnp.sum(weights, axis=2)), weighted), None)
        suffix_weights = jnp.where(suffix_valid, jnp.exp(suffix_scores - row_top[:, :, None]), 0.0)
        own_weights = jnp.exp(own_scores - row_top)
        weight_total = lax.optimization_barrier(jnp.sum(suffix_weights, axis=2)) + own_weights
        weighted = jnp.einsum('rgk,rkd->rgd', round_trip(suffix_weights), suffix_value)
        weighted = weighted + round_trip(own_weights)[:, :, None] * value_new[:, None, :]
        (weight_total, weighted), _ = lax.scan(sum_step, (weight_total, weighted), (key_blocks, value_blocks))
        return (weighted / weight_total[:, :, None]).astype(jnp.bfloat16).reshape(REQ, GROUP * HD)
    groups = lax.map(one_group, jnp.arange(KVH, dtype=jnp.int32))
    context = jnp.transpose(groups, (1, 0, 2)).reshape(REQ, KVH * GROUP * HD)
    attn_out = jnp.dot(context, w_out, preferred_element_type=jnp.float32).astype(jnp.bfloat16)
    return (context, attn_out, new_keys, new_values)
```

```python
import functools
import math

import jax
import jax.numpy as jnp
from jax import lax
from jax.experimental import pallas as pl
from jax.experimental.pallas import tpu as pltpu
from jax.sharding import PartitionSpec as P

bf16 = jnp.bfloat16
f32 = jnp.float32
big_negative = -1e30
EPS = 1e-05
VMEM_LIMIT = 48 * 2**20


def params():
    return pltpu.CompilerParams(vmem_limit_bytes=VMEM_LIMIT)


def bt(a, b):
    return lax.dot_general(a, b, (((1,), (1,)), ((), ())), preferred_element_type=f32)


def mm(a, b):
    return lax.dot_general(a, b, (((1,), (0,)), ((), ())), preferred_element_type=f32)


def prefix_kernel(q_ref, k_ref, v_ref, o_ref, lse_ref, vt_ref, *, span, scale):
    rows, width = q_ref.shape
    steps = k_ref.shape[0] // span
    q = q_ref[...]
    vt_ref[...] = v_ref[...].T
    top = jnp.full((1, rows), big_negative, f32)
    total = jnp.zeros((1, rows), f32)
    acc = jnp.zeros((width, rows), f32)
    for i in range(steps):
        s = bt(k_ref[i * span : (i + 1) * span, :], q) * scale
        new_top = jnp.maximum(top, jnp.max(s, axis=0, keepdims=True))
        p = jnp.exp(s - new_top)
        fade = jnp.exp(top - new_top)
        total = total * fade + jnp.sum(p, axis=0, keepdims=True)
        acc = acc * fade + mm(vt_ref[:, i * span : (i + 1) * span], p.astype(bf16))
        top = new_top
    o_ref[...] = (acc / total).T.astype(o_ref.dtype)
    lse_ref[...] = top + jnp.log(total)


def prefix_attention(q, k, v, scale, out_dtype):
    rows, width = q.shape
    span = 512
    return pl.pallas_call(
        functools.partial(prefix_kernel, span=span, scale=scale),
        out_shape=[
            jax.ShapeDtypeStruct((rows, width), out_dtype),
            jax.ShapeDtypeStruct((1, rows), f32),
        ],
        scratch_shapes=[pltpu.VMEM((v.shape[1], v.shape[0]), bf16)],
        compiler_params=params(),
        cost_estimate=pl.CostEstimate(
            flops=4 * rows * k.shape[0] * width,
            bytes_accessed=4 * k.shape[0] * width,
            transcendentals=rows * k.shape[0],
        ),
        name="prefix_attention",
    )(q, k, v)


def suffix_kernel(len_ref, q_ref, kn_ref, vn_ref, k_ref, v_ref, o_ref, lse_ref, *, group, scale):
    own, slots, width = k_ref.shape
    rows = own * group
    q = q_ref[...]
    own_score = jnp.sum(q.astype(f32) * kn_ref[...].astype(f32), axis=1, keepdims=True) * scale
    place = lax.broadcasted_iota(jnp.int32, (group, slots), 1)
    for r in range(own):
        at = slice(r * group, (r + 1) * group)
        s = bt(q[at], k_ref[r]) * scale
        usable = place < len_ref[r]
        s = jnp.where(usable, s, big_negative)
        top = jnp.maximum(jnp.max(s, axis=1, keepdims=True), own_score[at])
        p = jnp.where(usable, jnp.exp(s - top), 0.0)
        own_p = jnp.exp(own_score[at] - top)
        total = jnp.sum(p, axis=1, keepdims=True) + own_p
        acc = mm(p.astype(bf16), v_ref[r])
        acc = acc + own_p.astype(bf16).astype(f32) * vn_ref[at, :].astype(f32)
        o_ref[at, :] = acc / total
        lse_ref[at, :] = top + jnp.log(total)


def suffix_attention(lengths, q, k_new, v_new, k, v, group, scale):
    rows, width = q.shape
    vmem = pl.BlockSpec(memory_space=pltpu.VMEM)
    return pl.pallas_call(
        functools.partial(suffix_kernel, group=group, scale=scale),
        in_specs=[pl.BlockSpec(memory_space=pltpu.SMEM)] + [vmem] * 5,
        out_specs=[vmem] * 2,
        out_shape=[
            jax.ShapeDtypeStruct((rows, width), f32),
            jax.ShapeDtypeStruct((rows, 1), f32),
        ],
        compiler_params=params(),
        name="suffix_attention",
    )(lengths, q, k_new, v_new, k, v)


def split3(value):
    first = value.astype(bf16)
    rest = value - first.astype(f32)
    second = rest.astype(bf16)
    third = (rest - second.astype(f32)).astype(bf16)
    return first, second, third


def swap(blocks, axis):
    return lax.all_to_all(blocks, axis, 0, 0, tiled=False)


def spread(block, axis):
    count = lax.axis_size(axis)
    return swap(jnp.broadcast_to(block[None], (count,) + block.shape), axis)


def local(
    token_ids,
    lengths,
    embed_table,
    norm_gain,
    w_query,
    w_key,
    w_value,
    prefix_keys,
    prefix_values,
    suffix_keys,
    suffix_values,
    w_out,
):
    toks = lax.axis_size("tok")
    groups = lax.axis_size("kvh")
    tok = lax.axis_index("tok")
    requests = token_ids.shape[0]
    own = requests // toks
    width = prefix_keys.shape[2]
    columns = w_query.shape[1]
    group = columns // width
    scale = 1.0 / math.sqrt(width)
    model = norm_gain.shape[0] * toks

    vocab = embed_table.shape[0]
    ids = token_ids - lax.axis_index("kvh") * vocab
    inside = (ids >= 0) & (ids < vocab)
    looked = jnp.take(embed_table, jnp.clip(ids, 0, vocab - 1), axis=0)
    picked = jnp.where(inside[:, None], looked, jnp.zeros((), bf16))
    pieces = swap(picked.reshape(groups, requests // groups, picked.shape[1]), "kvh")
    piece = jnp.sum(pieces.astype(f32), axis=0).astype(bf16)
    hidden = spread(piece, "kvh").reshape(picked.shape).astype(f32)

    squares = jnp.sum(hidden * hidden, axis=1, keepdims=True)
    scaled = (hidden * norm_gain.astype(f32)).astype(bf16)
    parts = jnp.concatenate(
        [
            mm(scaled, w_query),
            mm(scaled, w_key),
            mm(scaled, w_value),
            jnp.broadcast_to(squares, (requests, width)),
        ],
        axis=1,
    )
    sums = jnp.sum(swap(parts.reshape(toks, own, parts.shape[1]), "tok"), axis=0)
    inverse = lax.rsqrt(sums[:, columns + 2 * width :][:, :1] / model + EPS)
    own_all = (sums[:, : columns + 2 * width] * inverse).astype(bf16)
    own_query = own_all[:, :columns]
    own_key = own_all[:, columns : columns + width]
    own_value = own_all[:, columns + width :]

    queries = spread(own_query.reshape(own * group, width), "tok").reshape(requests * group, width)

    own_rows = own_query.reshape(own * group, width)
    own_lengths = lax.dynamic_slice_in_dim(lengths, tok * own, own, 0)
    tail_mean, tail_lse = suffix_attention(
        own_lengths,
        own_rows,
        jnp.repeat(own_key, group, axis=0),
        jnp.repeat(own_value, group, axis=0),
        suffix_keys[:, 0],
        suffix_values[:, 0],
        group,
        scale,
    )

    mean, lse = prefix_attention(queries, prefix_keys[0], prefix_values[0], scale, f32)
    rows = own * group
    packed = jnp.concatenate(
        [
            mean.reshape(toks, rows, width),
            jnp.pad(lse.reshape(toks, 1, rows), ((0, 0), (0, 0), (0, width - rows))),
        ],
        axis=1,
    )
    got = swap(packed, "tok")
    got_mean = got[:, :rows]
    got_lse = got[:, rows, :rows]
    top = jnp.maximum(jnp.max(got_lse, axis=0), tail_lse[:, 0])
    share = jnp.exp(got_lse - top)
    tail_share = jnp.exp(tail_lse[:, 0] - top)
    total = jnp.sum(share, axis=0) + tail_share
    blend = jnp.sum(got_mean * share[:, :, None], axis=0) + tail_mean * tail_share[:, None]
    context_own = (blend / total[:, None]).astype(bf16).reshape(own, columns)

    context = spread(context_own, "tok").reshape(requests, columns)
    out = mm(context, w_out).astype(bf16)
    out = swap(out.reshape(groups, requests // groups, out.shape[1]), "kvh")
    attn_out = jnp.sum(out.astype(f32), axis=0).astype(bf16)
    return (context_own, attn_out, own_key, own_value)


def solution(mesh):
    return jax.shard_map(
        local,
        mesh=mesh,
        in_specs=(
            P(),
            P(),
            P("kvh", "tok"),
            P("tok"),
            P("tok", "kvh"),
            P("tok", "kvh"),
            P("tok", "kvh"),
            P("kvh", "tok", None),
            P("kvh", "tok", None),
            P("tok", "kvh", None, None),
            P("tok", "kvh", None, None),
            P("kvh", "tok"),
        ),
        out_specs=(P("tok", "kvh"), P("kvh", "tok"), P("tok", "kvh"), P("tok", "kvh")),
        check_vma=False,
    )
```
